768 devices in a mesh: seq: 32 (over y_lo, x, core), tp: 24 (over z, y_hi).
Axes of the slice: x: 4, y: 8 (y_hi: 2, y_lo: 4; y = y_hi * 4 + y_lo), z: 12, core: 2. Of those that a mesh axis runs over, the one named last changes fastest.
Arguments:
- hidden: bfloat16 [4096, 8192], P('seq'), may hold values from -7 to 7
- norm_gain: bfloat16 [8192], replicated, may hold values from 0.099609375 to 1.8984375
- w_query: bfloat16 [8192, 6144], P('seq', 'tp'), may hold values from -1 to 1
- w_key: bfloat16 [8192, 768], P('seq'), may hold values from -64 to 64
- w_value: bfloat16 [8192, 768], P('seq'), may hold values from -0.0625 to 0.0625
- doc_lengths: int32 [8], replicated, may hold values from 1 to 2560, 4096 in all
- critic_up: bfloat16 [8192, 27648], P('seq', 'tp'), may hold values from -0.0625 to 0.0625
- critic_down: bfloat16 [4, 27648, 8192], P(None, 'tp', 'seq'), may hold values from -0.0390625 to 0.0390625
- rule_ids: int32 [8], replicated, may hold values from 0 to 3
Outputs:
- attention: bfloat16 [4096, 6144], P('seq', 'tp')
- critic_values: bfloat16 [8, 8192], P(None, 'seq')
The draws below stay inside these ranges and needn't reach their ends.
Inputs may be any that keep to these rules, and one draw needn't show every extreme that they name: `doc_lengths`: the 8 lengths sum to 4096; the longest is exactly 2560.
All inputs are finite; a program needn't handle non-finite values.
Results may differ from the reference program's by a relative error of at most 0.03.
The reference program's roundings to bfloat16 on the way (of `normed`, `end_rows` and `critic_hidden`) count: a program that leaves them out, or rounds other values in their place, can miss the bound.
Values may be sent and summed in bfloat16 or wider, within the bound.
A program may use at most 64 MiB of HBM per device.

```python
import math
import jax
import jax.numpy as jnp
import numpy as np
from jax import lax

D = 8192
HEAD = 128
GROUP = 8
DOCS = 8
RULES = 4
LEN = 4096
HEADS = 48
KV_HEADS = 6
CF = 27648


def query_table(key):
    base = jax.random.normal(jax.random.fold_in(key, 11), (D, HEADS * HEAD), jnp.float32)
    return jnp.clip(base, -4.0, 4.0) * (1.0 / math.sqrt(D))


def draw_w_query(key, part):
    return query_table(key).astype(jnp.bfloat16)


def draw_w_key(key, part):
    own = jax.random.normal(jax.random.fold_in(key, 12), (D, KV_HEADS * HEAD), jnp.float32)
    result = jnp.clip(own, -4.0, 4.0) * (1.0 / math.sqrt(D))
    return result.astype(jnp.bfloat16)


def draw_hidden(key, part):
    base = jnp.clip(jax.random.normal(jax.random.fold_in(key, 21), (LEN, D), jnp.float32), -6.0, 6.0)
    return base.astype(jnp.bfloat16)


def with_ends(values, own_key, least, largest):
    dims = values.shape
    spot = [jax.random.randint(jax.random.fold_in(own_key, axis), (), 0, dims[axis]) for axis in range(len(dims))]
    values = values.at[tuple(spot)].set(least)
    longest = dims.index(max(dims))
    spot[longest] = (spot[longest] + 1) % dims[longest]
    return values.at[tuple(spot)].set(largest)


def levels(key, shape, pieces, smallest, high):
    def one(axis_at, blocks):
        steps = jax.random.uniform(jax.random.fold_in(jax.random.fold_in(key, 6), axis_at), (blocks,), jnp.float32, smallest / len(pieces), high / len(pieces))
        return jnp.repeat(jnp.exp(steps), shape[axis_at] // blocks).reshape((-1,) + (1,) * (len(shape) - axis_at - 1))

    factor_of = one(*pieces[0])
    for cut in pieces[1:]:
        factor_of = factor_of * one(*cut)
    return factor_of


def split_up(number_of, total, limit, lean):
    weights = [(1 << 20) // math.isqrt(standing ** lean) + 1 for standing in range(2, number_of + 1)]
    spare, counts = total - limit - (number_of - 1), [1] * (number_of - 1)
    while spare > 0:
        candidates = [i for i in range(number_of - 1) if counts[i] < limit]
        pool, budget = sum([weights[i] for i in candidates]), spare
        for i in candidates:
            more = min(limit - counts[i], max(1, budget * weights[i] // pool), spare)
            counts[i] = counts[i] + more
            spare = spare - more
    return np.array([limit] + counts)


def ragged(rng, number_of, total, most, slope):
    if number_of == 2:
        one = jax.random.randint(rng, (), max(1, total - most), min(most, total - 1) + 1)
        return jnp.stack([one, total - one])
    tallies = jnp.asarray(split_up(number_of, total, most, slope), jnp.int32)
    pairs = (number_of - 1) // 2
    giver, taker = tallies[1:1 + 2 * pairs:2], tallies[2:2 + 2 * pairs:2]
    slack = jnp.minimum(giver - 1, most - taker)
    passed = jax.random.randint(jax.random.fold_in(rng, 1), (pairs,), 0, 1 << 20) % (slack + 1)
    tallies = tallies.at[1:1 + 2 * pairs:2].set(giver - passed).at[2:2 + 2 * pairs:2].set(taker + passed)
    return tallies[jax.random.permutation(jax.random.fold_in(rng, 2), number_of)]


def normal_values(rng, shape, scale, most, cuts=(), held_as=jnp.bfloat16):
    values = scale * jax.random.normal(rng, shape, jnp.float32)
    if cuts:
        values = values * levels(rng, shape, cuts, -0.22, 0.18)
    return jnp.clip(values, -most, most).astype(held_as)


def setup_inputs(seed: int = 0) -> dict:
    streams_of = jax.random.split(jax.random.key(seed), 10)
    hidden = draw_hidden(jax.random.fold_in(streams_of[9], 71), 0)
    norm_gain = jnp.clip(1.0 + 0.18 * jax.random.normal(streams_of[1], (D,), jnp.float32), 0.099609375, 1.8984375).astype(jnp.bfloat16)
    w_query = draw_w_query(jax.random.fold_in(streams_of[9], 71), 0)
    w_key = draw_w_key(jax.random.fold_in(streams_of[9], 71), 0)
    w_value = normal_values(streams_of[4], (D, KV_HEADS * HEAD), D ** -0.5, 0.0625, ((0, 32),))
    doc_lengths = ragged(streams_of[5], DOCS, LEN, LEN // 2 + LEN // 8, 2).astype(jnp.int32)
    critic_up = normal_values(streams_of[6], (D, CF), D ** -0.5, 0.0625, ((0, 32), (1, 24)))
    critic_down = normal_values(streams_of[7], (RULES, CF, D), CF ** -0.5, 0.0390625, ((1, 24), (2, 32)))
    rule_ids = with_ends(jax.random.randint(streams_of[8], (DOCS,), 0, RULES), jax.random.fold_in(streams_of[8], 1), 0, RULES - 1).astype(jnp.int32)
    return dict(hidden=hidden, norm_gain=norm_gain, w_query=w_query, w_key=w_key, w_value=w_value, doc_lengths=doc_lengths, critic_up=critic_up, critic_down=critic_down, rule_ids=rule_ids)


def rms_norm(values, norm_gain):
    widened = values.astype(jnp.float32)
    mean_square = lax.optimization_barrier(jnp.mean(widened * widened, axis=-1, keepdims=True))
    return (widened * lax.rsqrt(mean_square + 1e-05) * norm_gain.astype(jnp.float32)).astype(jnp.bfloat16)

def reference(hidden, norm_gain, w_query, w_key, w_value, doc_lengths, critic_up, critic_down, rule_ids):
    normed = rms_norm(hidden, norm_gain)
    queries = jnp.dot(normed, w_query, preferred_element_type=jnp.float32).astype(jnp.bfloat16).reshape(LEN, HEADS, HEAD)
    keys = jnp.dot(normed, w_key, preferred_element_type=jnp.float32).astype(jnp.bfloat16).reshape(LEN, KV_HEADS, HEAD)
    values = jnp.dot(normed, w_value, preferred_element_type=jnp.float32).astype(jnp.bfloat16).reshape(LEN, KV_HEADS, HEAD)
    doc_ends = (jnp.cumsum(doc_lengths) - 1).astype(jnp.int32)
    positions = jnp.arange(LEN, dtype=jnp.int32)
    segment = lax.optimization_barrier(jnp.sum((positions[:, None] > doc_ends[None, :]).astype(jnp.int32), axis=1))
    allowed = (segment[:, None] == segment[None, :]) & (positions[None, :] <= positions[:, None])
    inverse_root = 1.0 / math.sqrt(HEAD)

    def one_head(head):
        query_head = lax.dynamic_index_in_dim(queries, head, 1, keepdims=False)
        key_head = lax.dynamic_index_in_dim(keys, head // GROUP, 1, keepdims=False)
        value_head = lax.dynamic_index_in_dim(values, head // GROUP, 1, keepdims=False)
        scores = jnp.dot(query_head, key_head.T, preferred_element_type=jnp.float32) * inverse_root
        scores = jnp.where(allowed, scores, -1e+30)
        maxima = lax.optimization_barrier(jnp.max(scores, axis=1, keepdims=True))
        weights = jnp.where(allowed, jnp.exp(scores - maxima), 0.0)
        totals = lax.optimization_barrier(jnp.sum(weights, axis=1, keepdims=True))
        mixed = jnp.dot(weights.astype(jnp.bfloat16), value_head, preferred_element_type=jnp.float32)
        return mixed / totals
    heads_out = lax.map(one_head, jnp.arange(HEADS, dtype=jnp.int32))
    attention = jnp.transpose(heads_out, (1, 0, 2)).reshape(LEN, HEADS * HEAD).astype(jnp.bfloat16)
    end_rows = jnp.take(normed, doc_ends, axis=0)
    critic_hidden = jax.nn.silu(jnp.dot(end_rows, critic_up, preferred_element_type=jnp.float32)).astype(jnp.bfloat16)
    per_rule = jnp.einsum('dc,rce->dre', critic_hidden.astype(jnp.float32), critic_down.astype(jnp.float32))
    rule_pick = (rule_ids[:, None] == jnp.arange(RULES, dtype=jnp.int32)[None, :]).astype(jnp.float32)
    critic_values = jnp.einsum('dr,dre->de', rule_pick, per_rule).astype(jnp.bfloat16)
    return (attention, critic_values)
```

```python
import math

import jax
import jax.numpy as jnp
from jax import lax
from jax.experimental import pallas as pl
from jax.experimental.pallas import tpu as pltpu
from jax.sharding import PartitionSpec as P

QH_DEV = 2
GROUP = 8
NY, NX, NC = 4, 4, 2
NH = 2
KEY_CHUNK = 4
MESH = pl.DeviceIdType.MESH

EVENTS = (
    (0, 0), (1, 0), (0, -1), (0, 1), (2, 0), (3, 0), (1, -1), (1, 1),
    (2, -1), (2, 1), (3, -1), (3, 1), (0, 2), (1, 2), (2, 2), (3, 2),
)
N_SENDS = 31


def kernel(
    lens, rules, gain, hidden, w_query, w_key, w_value, critic_up, critic_down,
    attention, critic_values,
    hid, nrm, wkv, wq, up, down, kv, acc_kv, acc_q, scores,
    e0, ey, e1, ex, e2, es, u0, uy, u1, ux, u2, us, d0, dh, d1, dz,
    local, wkv_send, wkv_recv, wq_send, wq_recv, kv_send, kv_recv, kvz,
    e_send, e_recv, u_send, u_recv, d_send, d_recv,
):
    n_tp = lax.axis_size("tp")
    n_z = n_tp // NH
    tokens = hid.shape[0]
    docs = lens.shape[0]
    depth = wkv.shape[1]
    n_seq = NY * NX * NC
    s, t = lax.axis_index("seq"), lax.axis_index("tp")
    c, x, y = s % NC, s // NC % NX, s // (NC * NX)
    z, h = t // NH, t % NH

    def row(k):
        return (y // 2 + k // 2) % 2 * 2 + (y + k) % 2

    def slot(ay, ax, ac):
        return (ay * NX + ax) * NC + ac

    def column(dx):
        return (x + dx + NX) % NX

    sib = (slot(y, x, 1 - c), t)
    y_peer = [(slot(row(k), x, c), t) for k in range(NY)]
    x_peer = [(slot(y, column(j), c), t) for j in range(NX)]
    z_mate = (s, (z + 1 - 2 * (z % 2)) * NH + h)
    h_peer = (s, z * NH + 1 - h)
    z_peer = [(s, (z + j) % n_z * NH + h) for j in range(n_z)]

    head = pl.ds(pl.multiple_of((t * QH_DEV // GROUP) * 128, 128), 128)
    key_copy = pltpu.make_async_copy(w_key.at[:, head], wkv.at[s], local.at[0])
    value_copy = pltpu.make_async_copy(w_value.at[:, head], wkv.at[s], local.at[0])

    @pl.when(z % 2 == 0)
    def _():
        key_copy.start()

    @pl.when(z % 2 == 1)
    def _():
        value_copy.start()

    wq_copy = pltpu.make_async_copy(w_query, wq.at[s], local.at[1])
    hid_copy = pltpu.make_async_copy(hidden, hid, local.at[2])
    up_copy = pltpu.make_async_copy(critic_up, up, local.at[3])
    down_copy = pltpu.make_async_copy(critic_down, down, local.at[4])
    for copy in (wq_copy, hid_copy, up_copy, down_copy):
        copy.start()

    barrier = pltpu.get_barrier_semaphore()
    partners = [sib, *y_peer[1:], *x_peer[1:], h_peer, *z_peer[1:]]
    for partner in partners:
        pl.semaphore_signal(barrier, inc=1, device_id=partner, device_id_type=MESH)
    pl.semaphore_wait(barrier, len(partners))

    sends = []

    def remote(src, dst, send_sem, recv_sem, device):
        return pltpu.make_async_remote_copy(
            src_ref=src, dst_ref=dst, send_sem=send_sem, recv_sem=recv_sem,
            device_id=device, device_id_type=MESH,
        )

    def send(*args):
        copy = remote(*args)
        copy.start()
        sends.append(copy)

    def gather(buf, send_sems, recv_sems):
        def go(a, device, i):
            send(buf.at[a], buf.at[a], send_sems.at[i], recv_sems.at[a], device)

        def got(a):
            remote(buf.at[a], buf.at[a], send_sems.at[0], recv_sems.at[a], sib).wait_recv()

        def own(i):
            k, dx = EVENTS[i]
            a = slot(row(k), column(dx), c)
            if i > 0:
                got(a)
            else:
                for j in range(1, NY):
                    go(a, y_peer[j], j - 1)
            if dx == 0:
                go(a, x_peer[1], 3 + k)
                go(a, x_peer[3], 7 + k)
            if dx == -1 and k % 2 == 0:
                go(a, x_peer[1], 11 + k // 2)
            if dx == 1 and k % 2 == 1:
                go(a, x_peer[3], 13 + k // 2)
            go(a, sib, 15 + i)
            return a

        def other(i):
            k, dx = EVENTS[i]
            a = slot(row(k), column(dx), 1 - c)
            got(a)
            return a

        return own, other

    kvw_own, kvw_other = gather(wkv, wkv_send, wkv_recv)
    q_own, q_other = gather(wq, wq_send, wq_recv)
    value_copy.wait()
    kvw_own(0)
    wq_copy.wait()
    q_own(0)

    hid_copy.wait()
    wide_gain = gain[...].astype(jnp.float32)

    def norm_rows(i, carry):
        rows = pl.ds(pl.multiple_of(i * 16, 16), 16)
        wide = hid[rows, :].astype(jnp.float32)
        mean_square = jnp.mean(wide * wide, axis=-1, keepdims=True)
        normed = (wide * lax.rsqrt(mean_square + 1e-05) * wide_gain).astype(jnp.bfloat16)
        for a in range(n_seq):
            nrm[a, rows, :] = normed[:, a * depth : (a + 1) * depth]
        return carry

    lax.fori_loop(0, tokens // 16, norm_rows, 0)

    ends, run = [], 0
    for d in range(docs):
        run = run + lens[d]
        ends.append(run - 1)
    first = s * tokens
    doc_of = lax.broadcasted_iota(jnp.int32, (docs, tokens), 0)
    ends_vec = jnp.zeros((docs, tokens), jnp.int32)
    for d in range(docs):
        ends_vec = jnp.where(doc_of == d, ends[d], ends_vec)
    here = lax.broadcasted_iota(jnp.int32, (docs, tokens), 1) + first
    picker = (ends_vec == here).astype(jnp.float32).astype(jnp.bfloat16)

    def pick(a, carry):
        e0[a] = jnp.dot(picker, nrm[a], preferred_element_type=jnp.float32)
        return carry

    lax.fori_loop(0, n_seq, pick, 0)
    per_y = NX * NC
    for k in range(1, NY):
        send(
            e0.at[pl.ds(row(k) * per_y, per_y)], ey.at[k - 1], e_send.at[k - 1], e_recv.at[k - 1],
            y_peer[k],
        )

    def wait_for(ref, recv_sem, send_sem):
        remote(ref, ref, send_sem, recv_sem, sib).wait_recv()

    def end_rows_y():
        for k in range(NY - 1):
            wait_for(ey.at[k], e_recv.at[k], e_send.at[0])
        e1[...] = e0[pl.ds(y * per_y, per_y)] + ey[0] + ey[1] + ey[2]
        for j in range(1, NX):
            send(
                e1.at[pl.ds(column(j) * NC, NC)], ex.at[j - 1], e_send.at[2 + j], e_recv.at[2 + j],
                x_peer[j],
            )

    def end_rows_x():
        for j in range(NX - 1):
            wait_for(ex.at[j], e_recv.at[3 + j], e_send.at[0])
        e2[...] = e1[pl.ds(x * NC, NC)] + ex[0] + ex[1] + ex[2]
        send(e2.at[1 - c], es, e_send.at[6], e_recv.at[6], sib)

    def up_terms():
        wait_for(es, e_recv.at[6], e_send.at[0])
        end_rows = (e2[c] + es[...]).astype(jnp.bfloat16)
        up_copy.wait()
        u0[...] = jnp.dot(end_rows, up[...], preferred_element_type=jnp.float32)
        for k in range(1, NY):
            send(u0, uy.at[k - 1], u_send.at[k - 1], u_recv.at[k - 1], y_peer[k])

    def up_y():
        for k in range(NY - 1):
            wait_for(uy.at[k], u_recv.at[k], u_send.at[0])
        u1[...] = u0[...] + uy[0] + uy[1] + uy[2]
        for j in range(1, NX):
            send(u1, ux.at[j - 1], u_send.at[2 + j], u_recv.at[2 + j], x_peer[j])

    def up_x():
        for j in range(NX - 1):
            wait_for(ux.at[j], u_recv.at[3 + j], u_send.at[0])
        u2[...] = u1[...] + ux[0] + ux[1] + ux[2]
        send(u2, us, u_send.at[6], u_recv.at[6], sib)

    def down_terms():
        wait_for(us, u_recv.at[6], u_send.at[0])
        v = u2[...] + us[...]
        critic_hidden = v / (1.0 + jnp.exp(-v))
        doc = lax.broadcasted_iota(jnp.int32, critic_hidden.shape, 0)
        rule = jnp.zeros(critic_hidden.shape, jnp.int32)
        for d in range(docs):
            rule = jnp.where(doc == d, rules[d], rule)
        down_copy.wait()
        total = None
        for r in range(down.shape[0]):
            mine = jnp.where(rule == r, critic_hidden, 0.0).astype(jnp.bfloat16)
            term = jnp.dot(mine, down[r], preferred_element_type=jnp.float32)
            total = term if total is None else total + term
        d0[...] = total
        send(d0, dh, d_send.at[0], d_recv.at[n_z], h_peer)

    def down_h():
        wait_for(dh, d_recv.at[n_z], d_send.at[0])
        both = d0[...] + dh[...]
        d1[...] = both
        dz[z] = both
        for j in range(1, n_z):
            send(d1, dz.at[z], d_send.at[j], d_recv.at[z], z_peer[j])

    def down_z():
        for j in range(1, n_z):
            there = (z + j) % n_z
            wait_for(dz.at[there], d_recv.at[there], d_send.at[0])
        total = dz[0]
        for a in range(1, n_z):
            total = total + dz[a]
        critic_values[...] = total.astype(jnp.bfloat16)

    acc_kv[...] = jnp.zeros_like(acc_kv)
    acc_q[...] = jnp.zeros_like(acc_q)

    def use_kv(a):
        acc_kv[...] += jnp.dot(nrm[a], wkv[a], preferred_element_type=jnp.float32)

    def use_q(a):
        acc_q[...] += jnp.dot(nrm[a], wq[a], preferred_element_type=jnp.float32)

    n_events = len(EVENTS)
    use_kv(s)
    stages = {5: end_rows_y, 9: end_rows_x, 13: up_terms}
    for i in range(1, n_events):
        use_kv(kvw_own(i))
        if i >= 2:
            use_kv(kvw_other(i - 2))
        if i in stages:
            stages[i]()
    use_kv(kvw_other(n_events - 2))
    use_kv(kvw_other(n_events - 1))
    kind = z % 2
    kv[s, kind] = acc_kv[...].astype(jnp.bfloat16)
    send(kv.at[s, kind], kv.at[s, kind], kvz.at[0], kvz.at[1], z_mate)

    kv_own, kv_other = gather(kv, kv_send, kv_recv)
    use_q(s)
    stages = {3: up_y, 6: up_x, 9: down_terms, 12: down_h}
    lead = 4
    for i in range(1, n_events + lead):
        if i < n_events:
            use_q(q_own(i))
            if i >= 2:
                use_q(q_other(i - 2))
        if i == lead:
            wait_for(kv.at[s, 1 - kind], kvz.at[1], kvz.at[0])
        if i >= lead:
            kv_own(i - lead)
        if i in stages:
            stages[i]()
    use_q(q_other(n_events - 2))
    use_q(q_other(n_events - 1))
    for i in range(n_events):
        kv_other(i)

    queries = acc_q[...].astype(jnp.bfloat16)
    stacked = jnp.concatenate([queries[:, :128], queries[:, 128:]], axis=0)
    rows = QH_DEV * tokens
    position = lax.broadcasted_iota(jnp.int32, (rows, 1), 0) % tokens + first
    start = jnp.zeros((rows, 1), jnp.int32)
    for d in range(docs):
        start = jnp.maximum(start, jnp.where(ends[d] < position, ends[d] + 1, 0))
    chunk = KEY_CHUNK * tokens
    chunks = s // KEY_CHUNK + 1
    inverse_root = 1.0 / math.sqrt(128)

    def score(i, maxima):
        keys = kv[pl.ds(i * KEY_CHUNK, KEY_CHUNK), 0].reshape(chunk, 128)
        found = lax.dot_general(
            stacked, keys, (((1,), (1,)), ((), ())), preferred_element_type=jnp.float32
        )
        there = lax.broadcasted_iota(jnp.int32, (rows, chunk), 1) + i * chunk
        allowed = (there >= start) & (there <= position)
        found = jnp.where(allowed, found * inverse_root, -1e30)
        scores[i] = found
        return jnp.maximum(maxima, jnp.max(found, axis=1, keepdims=True))

    maxima = lax.fori_loop(0, chunks, score, jnp.full((rows, 1), -1e30, jnp.float32))

    def mix(i, carry):
        totals, mixed = carry
        values = kv[pl.ds(i * KEY_CHUNK, KEY_CHUNK), 1].reshape(chunk, 128)
        weights = jnp.exp(scores[i] - maxima)
        totals = totals + jnp.sum(weights, axis=1, keepdims=True)
        mixed = mixed + jnp.dot(
            weights.astype(jnp.bfloat16), values, preferred_element_type=jnp.float32
        )
        return totals, mixed

    totals, mixed = lax.fori_loop(
        0, chunks, mix, (jnp.zeros((rows, 1), jnp.float32), jnp.zeros((rows, 128), jnp.float32))
    )
    out = (mixed / totals).astype(jnp.bfloat16)
    attention[:, :128] = out[:tokens]
    attention[:, 128:] = out[tokens:]
    down_z()
    for copy in sends:
        copy.wait_send()


def shards(
    hidden, norm_gain, w_query, w_key, w_value, doc_lengths, critic_up, critic_down, rule_ids
):
    tokens, width = hidden.shape
    depth, q_columns = w_query.shape
    rules, hidden_units, out_columns = critic_down.shape
    docs = doc_lengths.shape[0]
    n_seq = NY * NX * NC
    n_z = lax.axis_size("tp") // NH
    bf16, f32 = jnp.bfloat16, jnp.float32
    vmem, dma = pltpu.VMEM, pltpu.SemaphoreType.DMA
    anywhere = pl.BlockSpec(memory_space=pl.ANY)
    return pl.pallas_call(
        kernel,
        out_shape=(
            jax.ShapeDtypeStruct((tokens, q_columns), bf16),
            jax.ShapeDtypeStruct((docs, out_columns), bf16),
        ),
        in_specs=[
            pl.BlockSpec(memory_space=pltpu.SMEM),
            pl.BlockSpec(memory_space=pltpu.SMEM),
            pl.BlockSpec(memory_space=pltpu.VMEM),
            *[anywhere] * 6,
        ],
        out_specs=(pl.BlockSpec(memory_space=pltpu.VMEM), pl.BlockSpec(memory_space=pltpu.VMEM)),
        scratch_shapes=[
            vmem((tokens, width), bf16),
            vmem((n_seq, tokens, depth), bf16),
            vmem((n_seq, depth, 128), bf16),
            vmem((n_seq, depth, q_columns), bf16),
            vmem(critic_up.shape, bf16),
            vmem(critic_down.shape, bf16),
            vmem((n_seq, 2, tokens, 128), bf16),
            vmem((tokens, 128), f32),
            vmem((tokens, q_columns), f32),
            vmem((n_seq // KEY_CHUNK, QH_DEV * tokens, KEY_CHUNK * tokens), f32),
            vmem((n_seq, docs, depth), f32),
            vmem((NY - 1, NX * NC, docs, depth), f32),
            vmem((NX * NC, docs, depth), f32),
            vmem((NX - 1, NC, docs, depth), f32),
            vmem((NC, docs, depth), f32),
            vmem((docs, depth), f32),
            vmem((docs, hidden_units), f32),
            vmem((NY - 1, docs, hidden_units), f32),
            vmem((docs, hidden_units), f32),
            vmem((NX - 1, docs, hidden_units), f32),
            vmem((docs, hidden_units), f32),
            vmem((docs, hidden_units), f32),
            vmem((docs, out_columns), f32),
            vmem((docs, out_columns), f32),
            vmem((docs, out_columns), f32),
            vmem((n_z, docs, out_columns), f32),
            dma((5,)),
            dma((N_SENDS,)),
            dma((n_seq,)),
            dma((N_SENDS,)),
            dma((n_seq,)),
            dma((N_SENDS,)),
            dma((n_seq,)),
            dma((2,)),
            dma((7,)),
            dma((7,)),
            dma((7,)),
            dma((7,)),
            dma((n_z,)),
            dma((n_z + 1,)),
        ],
        compiler_params=pltpu.CompilerParams(
            collective_id=0, has_side_effects=True, vmem_limit_bytes=60 * 1024 * 1024
        ),
        cost_estimate=pl.CostEstimate(
            flops=2 * 10**9, bytes_accessed=8 * 2**20, transcendentals=2**20
        ),
    )(
        doc_lengths, rule_ids, norm_gain.reshape(1, width), hidden, w_query, w_key, w_value,
        critic_up, critic_down,
    )


def solution(mesh):
    return jax.shard_map(
        shards,
        mesh=mesh,
        in_specs=(
            P("seq", None),
            P(),
            P("seq", "tp"),
            P("seq", None),
            P("seq", None),
            P(),
            P("seq", "tp"),
            P(None, "tp", "seq"),
            P(),
        ),
        out_specs=(P("seq", "tp"), P(None, "seq")),
        check_vma=False,
    )
```

```python
import functools
import math

import jax
import jax.numpy as jnp
from jax import lax
from jax.experimental import pallas as pl
from jax.experimental.pallas import tpu as pltpu
from jax.sharding import PartitionSpec as P

QH_DEV = 2
GROUP = 8
NY, NX, NC = 4, 4, 2
NH = 2
KEY_CHUNK = 4
MESH = pl.DeviceIdType.MESH

LINE_EVENTS = (
    (0, 0), (1, 0), (0, -1), (0, 1), (2, 0), (3, 0), (1, -1), (1, 1),
    (2, -1), (2, 1), (3, -1), (3, 1), (0, 2), (1, 2), (2, 2), (3, 2),
)
RING_EVENTS = (
    (0, 0), (-1, 0), (1, 0), (0, -1), (0, 1), (2, 0), (-1, -1), (-1, 1),
    (1, -1), (1, 1), (2, -1), (2, 1), (0, 2), (1, 2), (-1, 2), (2, 2),
)
N_SENDS = 32
SCHEDULE = (
    "w0", "q0", "ends", "w1", "w2", "w3", "late", "norm", "ey", "w4", "w5", "q1", "w6", "q2", "w7", "w8", "q3", "w9",
    "q4", "ex", "up", "w10", "w11", "q5", "w12", "both", "w13", "w14", "w15", "kpart", "uy", "q6", "q7", "kown", "ux",
    "z", "k0", "v0", "q8", "q9", "down", "k1", "k2", "q10", "v1", "v2", "q11", "v3", "q12", "q13", "k3", "k4", "k5",
    "v4", "k6", "q14", "v5", "k7", "v6", "dh", "q15", "qpart", "k8", "v7", "k9", "v8", "k10", "k11", "v9", "k12",
    "v10", "v11", "v12", "qown", "a0", "k13", "v13", "v14", "k14", "a1", "k15", "v15", "a2", "a3", "dz",
)


def kernel(
    lens, rules, gain, hidden, w_query, w_key, w_value, critic_up, critic_down,
    attention, critic_values,
    hid, both, outbox, wkv, wq, up, down, kv, acc_kv, part_kv, acc_q, part_q, stacked, maxima, totals, mixed,
    e0, ey, e1, ex, e2, es, picked, u0, uy, u1, ux, u2, us, d0, dh, d1, dz,
    local, w_send, w_recv, q_send, q_recv, k_send, k_recv, v_send, v_recv, kvz, swap,
    e_send, e_recv, u_send, u_recv, d_send, d_recv,
):
    f32, bf16 = jnp.float32, jnp.bfloat16
    n_z = lax.axis_size("tp") // NH
    tokens, width = hid.shape
    docs = lens.shape[0]
    depth = wkv.shape[1]
    n_seq = NY * NX * NC
    s, t = lax.axis_index("seq"), lax.axis_index("tp")
    c, x, y = s % NC, s // NC % NX, s // (NC * NX)
    z, h = t // NH, t % NH
    tall = h * NY + y
    here = y * NX + x

    def row(k):
        return (y // 2 + k // 2) % 2 * 2 + (y + k) % 2

    def slot(ay, ax, ac):
        return (ay * NX + ax) * NC + ac

    def column(dx):
        return (x + dx + NX) % NX

    def up_by(dy):
        there = (tall + dy + NH * NY) % (NH * NY)
        return (slot(there % NY, x, c), z * NH + there // NY)

    sib = (slot(y, x, 1 - c), t)
    y_peer = [(slot(row(k), x, c), t) for k in range(NY)]
    x_peer = [(slot(y, column(j), c), t) for j in range(NX)]
    x_next, x_back, y_next, y_back = x_peer[1], x_peer[3], up_by(1), up_by(-1)
    z_mate = (s, (z + 1 - 2 * (z % 2)) * NH + h)
    h_peer = up_by(NY)
    z_peer = [(s, (z + j) % n_z * NH + h) for j in range(n_z)]

    head = pl.ds(pl.multiple_of((t * QH_DEV // GROUP) * 128, 128), 128)
    key_copy = pltpu.make_async_copy(w_key.at[:, head], wkv.at[here], local.at[0])
    value_copy = pltpu.make_async_copy(w_value.at[:, head], wkv.at[here], local.at[0])

    @pl.when(z % 2 == 0)
    def _():
        key_copy.start()

    @pl.when(z % 2 == 1)
    def _():
        value_copy.start()

    wq_copy = pltpu.make_async_copy(w_query, wq.at[here], local.at[1])
    hid_copy = pltpu.make_async_copy(hidden, hid, local.at[2])
    up_copy = pltpu.make_async_copy(critic_up, up, local.at[3])
    down_copy = pltpu.make_async_copy(critic_down, down, local.at[4])
    for copy in (wq_copy, hid_copy):
        copy.start()

    barrier = pltpu.get_barrier_semaphore()
    partners = [
        sib, *y_peer[1:], *x_peer[1:], y_next, y_back, up_by(2), up_by(-2), h_peer, *z_peer[1:],
    ]
    for partner in partners:
        pl.semaphore_signal(barrier, inc=1, device_id=partner, device_id_type=MESH)
    pl.semaphore_wait(barrier, len(partners))

    sends = []

    def remote(src, dst, send_sem, recv_sem, device):
        return pltpu.make_async_remote_copy(
            src_ref=src, dst_ref=dst, send_sem=send_sem, recv_sem=recv_sem,
            device_id=device, device_id_type=MESH,
        )

    def send(*args, when=None):
        copy = remote(*args)
        sends.append((copy, when))
        if when is None:
            copy.start()
        else:
            pl.when(when)(copy.start)

    def wait_for(ref, recv_sem, send_sem):
        remote(ref, ref, send_sem, recv_sem, sib).wait_recv()

    def mover(buf, send_sems, recv_sems):
        used = []

        def go(a, device, part=None, when=None):
            ref = buf.at[a] if part is None else buf.at[a, part]
            send(ref, ref, send_sems.at[len(used)], recv_sems.at[a], device, when=when)
            used.append(a)

        def got(a):
            wait_for(buf.at[a], recv_sems.at[a], send_sems.at[0])

        return go, got

    upper = y // 2
    inner_row = y + upper * (3 - 2 * y)
    inside = inner_row == 1
    inward = (slot(y + 1 - 2 * upper, x, c), t)
    outward = (slot((y - 1 + 2 * upper + NY) % NY, x, c), t)

    def line_gather(buf, send_sems, recv_sems):
        go, got = mover(buf, send_sems, recv_sems)

        def line_row(e):
            there = (inner_row, 1 - inner_row, 2, 3)[e]
            return there + upper * (3 - 2 * there)

        def own(i):
            e, dx = LINE_EVENTS[i]
            a = line_row(e) * NX + column(dx)
            if i > 0:
                got(a)
            if dx == 0:
                if e == 0:
                    go(a, inward)
                if e == 1:
                    go(a, inward, when=inside)
                else:
                    go(a, outward, when=inside)
            if dx == 0 or (dx == -1 and e % 2 == 0):
                go(a, x_next)
            if dx == 0 or (dx == 1 and e % 2 == 1):
                go(a, x_back)
            return a

        return own

    def ring_gather(buf, send_sems, recv_sems, x_first, cores):
        go, got = mover(buf, send_sems, recv_sems)
        near, far = ((x_next, x_back), (y_next, y_back)) if x_first else ((y_next, y_back), (x_next, x_back))
        half = buf.shape[1] // 2

        def place(a, b, core):
            dx, dy = (a, b) if x_first else (b, a)
            at = (y + dy + NY) % NY * NX + column(dx)
            return at * NC + core if cores else at

        def own(i):
            a, b = RING_EVENTS[i]
            shard = place(a, b, c)
            if i > 0:
                got(shard)
            if b == 0:
                if a == 0:
                    go(shard, near[0])
                    go(shard, near[1])
                if a == -1:
                    go(shard, near[0], pl.ds(0, half))
                if a == 1:
                    go(shard, near[1], pl.ds(half, half))
            if b == 0 or (b == -1 and a in (0, 1)):
                go(shard, far[0])
            if b == 0 or (b == 1 and a in (-1, 2)):
                go(shard, far[1])
            if cores:
                go(shard, sib)
            return shard

        def other(i):
            shard = place(*RING_EVENTS[i], 1 - c)
            got(shard)
            return shard

        return own, other

    w_own, _ = ring_gather(wkv, w_send, w_recv, False, False)
    q_own = line_gather(wq, q_send, q_recv)
    k_own, k_other = ring_gather(kv.at[0], k_send, k_recv, True, True)
    v_own, v_other = ring_gather(kv.at[1], v_send, v_recv, True, True)
    n_events = len(RING_EVENTS)

    acc_kv[...] = jnp.zeros_like(acc_kv)
    acc_q[...] = jnp.zeros_like(acc_q)

    ends, run = [], 0
    for d in range(docs):
        run = run + lens[d]
        ends.append(run - 1)
    first = s * tokens
    wide_gain = gain[...].reshape(1, width).astype(f32)

    def rms(wide, gains):
        mean_square = jnp.mean(wide * wide, axis=-1, keepdims=True)
        return (wide * lax.rsqrt(mean_square + 1e-05) * gains).astype(bf16)

    def norm():
        def norm_rows(i, carry):
            rows = pl.ds(pl.multiple_of(i * 16, 16), 16)
            normed = rms(hid[rows, :].astype(f32), wide_gain)
            for a in range(n_seq // NC):
                pair = [normed[:, (a * NC + core) * depth : (a * NC + core + 1) * depth] for core in range(NC)]
                both[a, c, rows, :] = jnp.where(c == 0, pair[0], pair[1])
                outbox[a, rows, :] = jnp.where(c == 0, pair[1], pair[0])
            return carry

        lax.fori_loop(0, tokens // 16, norm_rows, 0)
        send(outbox, both.at[:, c], swap.at[0], swap.at[1], sib)

    def other_rows():
        wait_for(outbox, swap.at[1], swap.at[0])

    def late():
        up_copy.start()
        down_copy.start()

    def end_rows():
        hid_copy.wait()
        doc = lax.broadcasted_iota(jnp.int32, (docs, tokens), 0)
        doc_end = jnp.zeros((docs, tokens), jnp.int32)
        for d in range(docs):
            doc_end = jnp.where(doc == d, ends[d], doc_end)
        place_here = lax.broadcasted_iota(jnp.int32, (docs, tokens), 1) + first
        picker = (doc_end == place_here).astype(f32).astype(bf16)
        step = 1024

        def columns(i, carry):
            part = pl.ds(pl.multiple_of(i * step, step), step)
            picked[:, part] = jnp.dot(picker, hid[:, part], preferred_element_type=f32)
            return carry

        lax.fori_loop(0, width // step, columns, 0)
        normed = rms(picked[...], wide_gain).astype(f32)
        for ay in range(NY):
            for ax in range(NX):
                at = slot(ay, ax, 0) * depth
                pair = [normed[:, at + core * depth : at + (core + 1) * depth] for core in range(NC)]
                e0[ay, ax] = jnp.concatenate(pair, axis=0).astype(bf16)
        for j, device in enumerate((y_next, up_by(2), y_back)):
            send(e0.at[(y + j + 1) % NY], ey.at[j], e_send.at[j], e_recv.at[j], device)

    def add(parts):
        total = parts[0].astype(f32)
        for part in parts[1:]:
            total = total + part.astype(f32)
        return total

    def end_rows_y():
        for k in range(NY - 1):
            wait_for(ey.at[k], e_recv.at[k], e_send.at[0])
        e1[...] = add([e0[y], *(ey[k] for k in range(NY - 1))]).astype(bf16)
        for j in range(1, NX):
            send(e1.at[column(j)], ex.at[j - 1], e_send.at[2 + j], e_recv.at[2 + j], x_peer[j])

    def end_rows_x():
        for j in range(NX - 1):
            wait_for(ex.at[j], e_recv.at[3 + j], e_send.at[0])
        e2[...] = add([e1[x], *(ex[j] for j in range(NX - 1))]).astype(bf16)
        send(e2, es, e_send.at[6], e_recv.at[6], sib)

    units = up.shape[1]
    wide_half = u0.shape[1]

    def up_terms():
        wait_for(es, e_recv.at[6], e_send.at[0])
        pair = add([e2[...], es[...]])
        end_row = jnp.where(c == 0, pair[:docs], pair[docs:]).astype(bf16)
        up_copy.wait()
        terms = jnp.dot(end_row, up[...], preferred_element_type=f32)
        pad = jnp.zeros((docs, 2 * wide_half - units), f32)
        lower = jnp.concatenate([terms[:, wide_half:], pad], axis=1)
        u0[...] = jnp.concatenate([terms[:, :wide_half], lower], axis=0).astype(bf16)
        for k in range(1, NY):
            send(u0, uy.at[k - 1], u_send.at[k - 1], u_recv.at[k - 1], y_peer[k])

    def up_y():
        for k in range(NY - 1):
            wait_for(uy.at[k], u_recv.at[k], u_send.at[0])
        u1[...] = add([u0[...], *(uy[k] for k in range(NY - 1))]).astype(bf16)
        for j in range(1, NX):
            send(u1, ux.at[j - 1], u_send.at[2 + j], u_recv.at[2 + j], x_peer[j])

    def up_x():
        for j in range(NX - 1):
            wait_for(ux.at[j], u_recv.at[3 + j], u_send.at[0])
        u2[...] = add([u1[...], *(ux[j] for j in range(NX - 1))]).astype(bf16)
        send(u2, us, u_send.at[6], u_recv.at[6], sib)

    def down_terms():
        wait_for(us, u_recv.at[6], u_send.at[0])
        sums = add([u2[...], us[...]])
        v = jnp.concatenate([sums[:docs], sums[docs:, : units - wide_half]], axis=1)
        critic_hidden = v / (1.0 + jnp.exp(-v))
        doc = lax.broadcasted_iota(jnp.int32, critic_hidden.shape, 0)
        rule = jnp.zeros(critic_hidden.shape, jnp.int32)
        for d in range(docs):
            rule = jnp.where(doc == d, rules[d], rule)
        down_copy.wait()
        total = None
        for r in range(down.shape[0]):
            mine = jnp.where(rule == r, critic_hidden, 0.0).astype(bf16)
            term = jnp.dot(mine, down[r], preferred_element_type=f32)
            total = term if total is None else total + term
        d0[...] = total
        send(d0, dh, d_send.at[0], d_recv.at[n_z], h_peer)

    def down_h():
        wait_for(dh, d_recv.at[n_z], d_send.at[0])
        both = d0[...] + dh[...]
        both = jnp.concatenate([both[:, :128], both[:, 128:]], axis=0).astype(bf16)
        d1[...] = both
        dz[z] = both
        for j in range(1, n_z):
            send(d1, dz.at[z], d_send.at[j], d_recv.at[z], z_peer[j])

    def down_z():
        for j in range(1, n_z):
            there = (z + j) % n_z
            wait_for(dz.at[there], d_recv.at[there], d_send.at[0])
        total = add([dz[a] for a in range(n_z)])
        critic_values[...] = jnp.concatenate([total[:docs], total[docs:]], axis=1).astype(bf16)

    kind = z % 2

    def product(a, weights):
        return jnp.dot(both[a].reshape(NC * tokens, depth), weights[a], preferred_element_type=f32)

    def use_w(a):
        acc_kv[...] += product(a, wkv).reshape(acc_kv.shape)

    def use_q(a):
        acc_q[...] += product(a, wq).reshape(acc_q.shape)

    def kv_part():
        send(acc_kv.at[1 - c], part_kv, swap.at[2], swap.at[3], sib)

    def kv_own_kind():
        wait_for(part_kv, swap.at[3], swap.at[2])
        kv[kind, s] = (acc_kv[c] + part_kv[...]).astype(bf16)
        send(kv.at[kind, s], kv.at[kind, s], kvz.at[0], kvz.at[1], z_mate)

    def other_kind():
        wait_for(kv.at[1 - kind, s], kvz.at[1], kvz.at[0])

    def q_part():
        send(acc_q.at[1 - c], part_q, swap.at[4], swap.at[5], sib)

    def q_sum():
        wait_for(part_q, swap.at[5], swap.at[4])

    groups = tuple(
        tuple(i for i, event in enumerate(RING_EVENTS) if event[1] == dy) for dy in (0, -1, 1, 2)
    )
    rows = QH_DEV * tokens
    chunk = KEY_CHUNK * tokens
    inverse_root = 1.0 / math.sqrt(128)

    def attend(g):
        for i in groups[g]:
            k_other(i)
            v_other(i)
        if g == 0:
            queries = (acc_q[c] + part_q[...]).astype(bf16)
            stacked[:tokens] = queries[:, :128]
            stacked[tokens:] = queries[:, 128:]
            maxima[...] = jnp.full_like(maxima, -1e30)
            totals[...] = jnp.zeros_like(totals)
            mixed[...] = jnp.zeros_like(mixed)
        dy = (0, -1, 1, 2)[g]
        chip_row = (y + dy + NY) % NY

        def step(i, carry):
            at = chip_row * (NX * NC) + i * KEY_CHUNK
            keys = kv[0, pl.ds(at, KEY_CHUNK)].reshape(chunk, 128)
            values = kv[1, pl.ds(at, KEY_CHUNK)].reshape(chunk, 128)
            position = lax.broadcasted_iota(jnp.int32, (rows, 1), 0) % tokens + first
            start = jnp.zeros((rows, 1), jnp.int32)
            for d in range(docs):
                start = jnp.maximum(start, jnp.where(ends[d] < position, ends[d] + 1, 0))
            found = lax.dot_general(
                stacked[...], keys, (((1,), (1,)), ((), ())), preferred_element_type=f32
            )
            there = lax.broadcasted_iota(jnp.int32, (rows, chunk), 1) + at * tokens
            allowed = (there >= start) & (there <= position)
            found = jnp.where(allowed, found * inverse_root, -1e30)
            old = maxima[...]
            new = jnp.maximum(old, jnp.max(found, axis=1, keepdims=True))
            weights = jnp.where(allowed, jnp.exp(found - new[:, :1]), 0.0)
            keep = jnp.exp(old - new)
            maxima[...] = new
            totals[...] = totals[...] * keep + jnp.sum(weights, axis=1, keepdims=True)
            mixed[...] = mixed[...] * keep + jnp.dot(
                weights.astype(bf16), values, preferred_element_type=f32
            )
            return carry

        steps = NX * NC // KEY_CHUNK
        if g == 0:
            lax.fori_loop(0, x * NC // KEY_CHUNK + 1, step, 0)
        else:

            @pl.when(chip_row < y)
            def _():
                lax.fori_loop(0, steps, step, 0)

    value_copy.wait()
    wq_copy.wait()
    waiting, ready = [], [False]

    def use(what, a):
        if ready[0]:
            what(a)
        else:
            waiting.append((what, a))

    stages = {
        "ends": end_rows, "norm": norm, "ey": end_rows_y, "ex": end_rows_x, "up": up_terms, "uy": up_y,
        "ux": up_x, "down": down_terms, "dh": down_h, "late": late, "both": other_rows, "kpart": kv_part,
        "kown": kv_own_kind, "z": other_kind, "qpart": q_part, "qown": q_sum,
        **{f"a{g}": functools.partial(attend, g) for g in range(4)}, "dz": down_z,
    }
    for step in SCHEDULE:
        if step in stages:
            stages[step]()
            if step == "both":
                ready[0] = True
                for what, a in waiting:
                    what(a)
            continue
        i = int(step[1:])
        if step[0] == "w":
            use(use_w, w_own(i))
        if step[0] == "q":
            use(use_q, q_own(i))
        if step[0] == "k":
            k_own(i)
        if step[0] == "v":
            v_own(i)
    out = (mixed[...] / totals[...]).astype(bf16)
    attention[:, :128] = out[:tokens]
    attention[:, 128:] = out[tokens:]
    for copy, when in sends:
        if when is None:
            copy.wait_send()
        else:
            pl.when(when)(copy.wait_send)


def hand_over(attention, critic_values, attention_out, critic_values_out):
    attention_out[...] = attention[...]
    critic_values_out[...] = critic_values[...]


def shards(
    hidden, norm_gain, w_query, w_key, w_value, doc_lengths, critic_up, critic_down, rule_ids
):
    tokens, width = hidden.shape
    depth, q_columns = w_query.shape
    rules, hidden_units, out_columns = critic_down.shape
    docs = doc_lengths.shape[0]
    n_seq = NY * NX * NC
    n_z = lax.axis_size("tp") // NH
    folded = (2 * docs, (hidden_units // 2 + 127) // 128 * 128)
    bf16, f32 = jnp.bfloat16, jnp.float32
    vmem, dma = pltpu.VMEM, pltpu.SemaphoreType.DMA
    anywhere = pl.BlockSpec(memory_space=pl.ANY)
    made = pl.pallas_call(
        kernel,
        out_shape=(
            jax.ShapeDtypeStruct((tokens, q_columns), bf16),
            jax.ShapeDtypeStruct((docs, out_columns), bf16),
        ),
        in_specs=[
            pl.BlockSpec(memory_space=pltpu.SMEM),
            pl.BlockSpec(memory_space=pltpu.SMEM),
            pl.BlockSpec(memory_space=pltpu.VMEM),
            *[anywhere] * 6,
        ],
        out_specs=(pl.BlockSpec(memory_space=pltpu.VMEM), pl.BlockSpec(memory_space=pltpu.VMEM)),
        scratch_shapes=[
            vmem((tokens, width), bf16),
            vmem((n_seq // NC, NC, tokens, depth), bf16),
            vmem((n_seq // NC, tokens, depth), bf16),
            vmem((n_seq // NC, depth, 128), bf16),
            vmem((n_seq // NC, depth, q_columns), bf16),
            vmem(critic_up.shape, bf16),
            vmem(critic_down.shape, bf16),
            vmem((2, n_seq, tokens, 128), bf16),
            vmem((NC, tokens, 128), f32),
            vmem((tokens, 128), f32),
            vmem((NC, tokens, q_columns), f32),
            vmem((tokens, q_columns), f32),
            vmem((QH_DEV * tokens, 128), bf16),
            *[vmem((QH_DEV * tokens, 128), f32)] * 3,
            vmem((NY, NX, NC * docs, depth), bf16),
            vmem((NY - 1, NX, NC * docs, depth), bf16),
            vmem((NX, NC * docs, depth), bf16),
            vmem((NX - 1, NC * docs, depth), bf16),
            vmem((NC * docs, depth), bf16),
            vmem((NC * docs, depth), bf16),
            vmem((docs, width), f32),
            vmem(folded, bf16),
            vmem((NY - 1, *folded), bf16),
            vmem(folded, bf16),
            vmem((NX - 1, *folded), bf16),
            vmem(folded, bf16),
            vmem(folded, bf16),
            vmem((docs, out_columns), f32),
            vmem((docs, out_columns), f32),
            vmem((2 * docs, out_columns // 2), bf16),
            vmem((n_z, 2 * docs, out_columns // 2), bf16),
            dma((5,)),
            *[dma((N_SENDS,)), dma((n_seq,))] * 4,
            dma((2,)),
            dma((6,)),
            dma((7,)),
            dma((7,)),
            dma((7,)),
            dma((7,)),
            dma((n_z,)),
            dma((n_z + 1,)),
        ],
        compiler_params=pltpu.CompilerParams(
            collective_id=0, has_side_effects=True, vmem_limit_bytes=60 * 1024 * 1024
        ),
        cost_estimate=pl.CostEstimate(
            flops=2 * 10**9, bytes_accessed=8 * 2**20, transcendentals=2**20
        ),
    )(
        doc_lengths, rule_ids, norm_gain, hidden, w_query, w_key, w_value,
        critic_up, critic_down,
    )
    inside = pl.BlockSpec(memory_space=pltpu.VMEM)
    return pl.pallas_call(
        hand_over,
        out_shape=tuple(jax.ShapeDtypeStruct(part.shape, part.dtype) for part in made),
        in_specs=[inside, inside],
        out_specs=(inside, inside),
    )(*made)


def solution(mesh):
    return jax.shard_map(
        shards,
        mesh=mesh,
        in_specs=(
            P("seq", None),
            P(),
            P("seq", "tp"),
            P("seq", None),
            P("seq", None),
            P(),
            P("seq", "tp"),
            P(None, "tp", "seq"),
            P(),
        ),
        out_specs=(P("seq", "tp"), P(None, "seq")),
        check_vma=False,
    )
```

```python
import functools
import math

import jax
import jax.numpy as jnp
from jax import lax
from jax.experimental import pallas as pl
from jax.experimental.pallas import tpu as pltpu
from jax.sharding import PartitionSpec as P

QH_DEV = 2
GROUP = 8
NY, NX, NC = 4, 4, 2
NH = 2
MESH = pl.DeviceIdType.MESH

LINE_EVENTS = (
    (0, 0), (1, 0), (0, -1), (0, 1), (2, 0), (3, 0), (1, -1), (1, 1),
    (2, -1), (2, 1), (3, -1), (3, 1), (0, 2), (1, 2), (2, 2), (3, 2),
)
RING_EVENTS = (
    (0, 0), (-1, 0), (1, 0), (0, -1), (0, 1), (2, 0), (-1, -1), (-1, 1),
    (1, -1), (1, 1), (2, -1), (2, 1), (0, 2), (1, 2), (-1, 2), (2, 2),
)
FAR = (0, -1, 1, 2)
LAST_OF = tuple(max(i for i, event in enumerate(RING_EVENTS) if event[1] == b) for b in FAR)
N_SENDS = 32
SCHEDULE = (
    "w0", "q0", "ends", "w1", "w2", "w3", "late", "norm", "ey", "w4", "w5", "q1", "w6", "q2", "w7", "w8", "q3", "w9",
    "q4", "ex", "up", "w10", "w11", "q5", "w12", "both", "w13", "w14", "w15", "kpart", "uy", "q6", "q7", "kown", "k0",
    "ux", "z", "v0", "q8", "q9", "down", "k1", "k2", "q10", "v1", "v2", "q11", "v3", "q12", "q13", "k3", "k4", "k5",
    "v4", "k6", "q14", "v5", "k7", "v6", "dh", "q15", "qpart", "k8", "v7", "k9", "v8", "k10", "k11", "v9", "k12",
    "v10", "v11", "v12", "qown", "a0", "k13", "v13", "v14", "k14", "a1", "k15", "v15", "a2", "a3", "dz",
)


def kernel(
    lens, rules, gain, hidden, w_query, w_key, w_value, critic_up, critic_down,
    attention, critic_values,
    hid, both, outbox, wkv, wq, up, down, kv, acc_kv, part_kv, acc_q, part_q, stacked, maxima, totals, mixed,
    e0, ey, e1, ex, e2, es, picked, u0, uy, u1, ux, u2, us, d0, dh, d1, dz,
    local, w_send, w_recv, q_send, q_recv, k_send, k_recv, v_send, v_recv, k_swap, v_swap, kvz, swap,
    e_send, e_recv, u_send, u_recv, d_send, d_recv,
):
    f32, bf16 = jnp.float32, jnp.bfloat16
    n_z = lax.axis_size("tp") // NH
    tokens, width = hid.shape
    docs = lens.shape[0]
    depth = wkv.shape[1]
    n_seq = NY * NX * NC
    s, t = lax.axis_index("seq"), lax.axis_index("tp")
    c, x, y = s % NC, s // NC % NX, s // (NC * NX)
    z, h = t // NH, t % NH
    tall = h * NY + y
    here = y * NX + x

    def row(k):
        return (y // 2 + k // 2) % 2 * 2 + (y + k) % 2

    def slot(ay, ax, ac):
        return (ay * NX + ax) * NC + ac

    def column(dx):
        return (x + dx + NX) % NX

    def up_by(dy):
        there = (tall + dy + NH * NY) % (NH * NY)
        return (slot(there % NY, x, c), z * NH + there // NY)

    sib = (slot(y, x, 1 - c), t)
    y_peer = [(slot(row(k), x, c), t) for k in range(NY)]
    x_peer = [(slot(y, column(j), c), t) for j in range(NX)]
    x_next, x_back, y_next, y_back = x_peer[1], x_peer[3], up_by(1), up_by(-1)
    z_mate = (s, (z + 1 - 2 * (z % 2)) * NH + h)
    h_peer = up_by(NY)
    z_peer = [(s, (z + j) % n_z * NH + h) for j in range(n_z)]

    head = pl.ds(pl.multiple_of((t * QH_DEV // GROUP) * 128, 128), 128)
    key_copy = pltpu.make_async_copy(w_key.at[:, head], wkv.at[here], local.at[0])
    value_copy = pltpu.make_async_copy(w_value.at[:, head], wkv.at[here], local.at[0])

    @pl.when(z % 2 == 0)
    def _():
        key_copy.start()

    @pl.when(z % 2 == 1)
    def _():
        value_copy.start()

    wq_copy = pltpu.make_async_copy(w_query, wq.at[here], local.at[1])
    hid_copy = pltpu.make_async_copy(hidden, hid, local.at[2])
    up_copy = pltpu.make_async_copy(critic_up, up, local.at[3])
    down_copy = pltpu.make_async_copy(critic_down, down, local.at[4])
    for copy in (wq_copy, hid_copy):
        copy.start()

    barrier = pltpu.get_barrier_semaphore()
    partners = [
        sib, *y_peer[1:], *x_peer[1:], y_next, y_back, up_by(2), up_by(-2), h_peer, *z_peer[1:],
    ]
    for partner in partners:
        pl.semaphore_signal(barrier, inc=1, device_id=partner, device_id_type=MESH)
    pl.semaphore_wait(barrier, len(partners))

    sends = []

    def remote(src, dst, send_sem, recv_sem, device):
        return pltpu.make_async_remote_copy(
            src_ref=src, dst_ref=dst, send_sem=send_sem, recv_sem=recv_sem,
            device_id=device, device_id_type=MESH,
        )

    def send(*args, when=None):
        copy = remote(*args)
        sends.append((copy, when))
        if when is None:
            copy.start()
        else:
            pl.when(when)(copy.start)

    def wait_for(ref, recv_sem, send_sem):
        remote(ref, ref, send_sem, recv_sem, sib).wait_recv()

    def mover(buf, send_sems, recv_sems):
        used = []

        def go(a, device, part=None, when=None):
            ref = buf.at[a] if part is None else buf.at[a, part]
            send(ref, ref, send_sems.at[len(used)], recv_sems.at[a], device, when=when)
            used.append(a)

        def got(a):
            wait_for(buf.at[a], recv_sems.at[a], send_sems.at[0])

        return go, got

    upper = y // 2
    inner_row = y + upper * (3 - 2 * y)
    inside = inner_row == 1
    inward = (slot(y + 1 - 2 * upper, x, c), t)
    outward = (slot((y - 1 + 2 * upper + NY) % NY, x, c), t)

    def line_gather(buf, send_sems, recv_sems):
        go, got = mover(buf, send_sems, recv_sems)

        def line_row(e):
            there = (inner_row, 1 - inner_row, 2, 3)[e]
            return there + upper * (3 - 2 * there)

        def own(i):
            e, dx = LINE_EVENTS[i]
            a = line_row(e) * NX + column(dx)
            if i > 0:
                got(a)
            if dx == 0:
                if e == 0:
                    go(a, inward)
                if e == 1:
                    go(a, inward, when=inside)
                else:
                    go(a, outward, when=inside)
            if dx == 0 or (dx == -1 and e % 2 == 0):
                go(a, x_next)
            if dx == 0 or (dx == 1 and e % 2 == 1):
                go(a, x_back)
            return a

        return own

    def ring_gather(buf, send_sems, recv_sems, x_first, swap_sems=None):
        go, got = mover(buf, send_sems, recv_sems)
        near, far = ((x_next, x_back), (y_next, y_back)) if x_first else ((y_next, y_back), (x_next, x_back))
        half = buf.shape[1] // 2

        def place(a, b, core):
            dx, dy = (a, b) if x_first else (b, a)
            ay, ax = (y + dy + NY) % NY, column(dx)
            return ay * NX + ax if swap_sems is None else (ay * NC + core) * NX + ax

        def line_of(b, core):
            return buf.at[pl.ds(((y + b + NY) % NY * NC + core) * NX, NX)]

        def own(i):
            a, b = RING_EVENTS[i]
            shard = place(a, b, c)
            if i > 0:
                got(shard)
            if b == 0:
                if a == 0:
                    go(shard, near[0])
                    go(shard, near[1])
                if a == -1:
                    go(shard, near[0], pl.ds(0, half))
                if a == 1:
                    go(shard, near[1], pl.ds(half, half))
            if b == 0 or (b == -1 and a in (0, 1)):
                go(shard, far[0])
            if b == 0 or (b == 1 and a in (-1, 2)):
                go(shard, far[1])
            if swap_sems is not None and i in LAST_OF:
                g = LAST_OF.index(i)
                line = line_of(FAR[g], c)
                send(line, line, swap_sems.at[g], swap_sems.at[len(FAR) + g], sib)
            return shard

        def other(g):
            wait_for(line_of(FAR[g], 1 - c), swap_sems.at[len(FAR) + g], swap_sems.at[g])

        return own, other

    kind = z % 2
    w_own, _ = ring_gather(wkv, w_send, w_recv, False)
    q_own = line_gather(wq, q_send, q_recv)
    k_own, k_other = ring_gather(kv.at[kind], k_send, k_recv, True, k_swap)
    v_own, v_other = ring_gather(kv.at[1 - kind], v_send, v_recv, True, v_swap)
    n_events = len(RING_EVENTS)

    acc_kv[...] = jnp.zeros_like(acc_kv)
    acc_q[...] = jnp.zeros_like(acc_q)

    ends, run = [], 0
    for d in range(docs):
        run = run + lens[d]
        ends.append(run - 1)
    first = s * tokens
    wide_gain = gain[...].reshape(1, width).astype(f32)

    def rms(wide, gains):
        mean_square = jnp.mean(wide * wide, axis=-1, keepdims=True)
        return (wide * lax.rsqrt(mean_square + 1e-05) * gains).astype(bf16)

    def norm():
        def norm_rows(i, carry):
            rows = pl.ds(pl.multiple_of(i * 16, 16), 16)
            normed = rms(hid[rows, :].astype(f32), wide_gain)
            for a in range(n_seq // NC):
                pair = [normed[:, (a * NC + core) * depth : (a * NC + core + 1) * depth] for core in range(NC)]
                both[a, c, rows, :] = jnp.where(c == 0, pair[0], pair[1])
                outbox[a, rows, :] = jnp.where(c == 0, pair[1], pair[0])
            return carry

        lax.fori_loop(0, tokens // 16, norm_rows, 0)
        send(outbox, both.at[:, c], swap.at[0], swap.at[1], sib)

    def other_rows():
        wait_for(outbox, swap.at[1], swap.at[0])

    def late():
        up_copy.start()
        down_copy.start()

    def end_rows():
        hid_copy.wait()
        doc = lax.broadcasted_iota(jnp.int32, (docs, tokens), 0)
        doc_end = jnp.zeros((docs, tokens), jnp.int32)
        for d in range(docs):
            doc_end = jnp.where(doc == d, ends[d], doc_end)
        place_here = lax.broadcasted_iota(jnp.int32, (docs, tokens), 1) + first
        picker = (doc_end == place_here).astype(f32).astype(bf16)
        step = 1024

        def columns(i, carry):
            part = pl.ds(pl.multiple_of(i * step, step), step)
            picked[:, part] = jnp.dot(picker, hid[:, part], preferred_element_type=f32)
            return carry

        lax.fori_loop(0, width // step, columns, 0)
        normed = rms(picked[...], wide_gain).astype(f32)
        for ay in range(NY):
            for ax in range(NX):
                at = slot(ay, ax, 0) * depth
                pair = [normed[:, at + core * depth : at + (core + 1) * depth] for core in range(NC)]
                e0[ay, ax] = jnp.concatenate(pair, axis=0).astype(bf16)
        for j, device in enumerate((y_next, up_by(2), y_back)):
            send(e0.at[(y + j + 1) % NY], ey.at[j], e_send.at[j], e_recv.at[j], device)

    def add(parts):
        total = parts[0].astype(f32)
        for part in parts[1:]:
            total = total + part.astype(f32)
        return total

    def end_rows_y():
        for k in range(NY - 1):
            wait_for(ey.at[k], e_recv.at[k], e_send.at[0])
        e1[...] = add([e0[y], *(ey[k] for k in range(NY - 1))]).astype(bf16)
        for j in range(1, NX):
            send(e1.at[column(j)], ex.at[j - 1], e_send.at[2 + j], e_recv.at[2 + j], x_peer[j])

    def end_rows_x():
        for j in range(NX - 1):
            wait_for(ex.at[j], e_recv.at[3 + j], e_send.at[0])
        e2[...] = add([e1[x], *(ex[j] for j in range(NX - 1))]).astype(bf16)
        send(e2, es, e_send.at[6], e_recv.at[6], sib)

    units = up.shape[1]
    wide_half = u0.shape[1]

    def up_terms():
        wait_for(es, e_recv.at[6], e_send.at[0])
        pair = add([e2[...], es[...]])
        end_row = jnp.where(c == 0, pair[:docs], pair[docs:]).astype(bf16)
        up_copy.wait()
        terms = jnp.dot(end_row, up[...], preferred_element_type=f32)
        pad = jnp.zeros((docs, 2 * wide_half - units), f32)
        lower = jnp.concatenate([terms[:, wide_half:], pad], axis=1)
        u0[...] = jnp.concatenate([terms[:, :wide_half], lower], axis=0).astype(bf16)
        for k in range(1, NY):
            send(u0, uy.at[k - 1], u_send.at[k - 1], u_recv.at[k - 1], y_peer[k])

    def up_y():
        for k in range(NY - 1):
            wait_for(uy.at[k], u_recv.at[k], u_send.at[0])
        u1[...] = add([u0[...], *(uy[k] for k in range(NY - 1))]).astype(bf16)
        for j in range(1, NX):
            send(u1, ux.at[j - 1], u_send.at[2 + j], u_recv.at[2 + j], x_peer[j])

    def up_x():
        for j in range(NX - 1):
            wait_for(ux.at[j], u_recv.at[3 + j], u_send.at[0])
        u2[...] = add([u1[...], *(ux[j] for j in range(NX - 1))]).astype(bf16)
        send(u2, us, u_send.at[6], u_recv.at[6], sib)

    def down_terms():
        wait_for(us, u_recv.at[6], u_send.at[0])
        sums = add([u2[...], us[...]])
        v = jnp.concatenate([sums[:docs], sums[docs:, : units - wide_half]], axis=1)
        critic_hidden = v / (1.0 + jnp.exp(-v))
        doc = lax.broadcasted_iota(jnp.int32, critic_hidden.shape, 0)
        rule = jnp.zeros(critic_hidden.shape, jnp.int32)
        for d in range(docs):
            rule = jnp.where(doc == d, rules[d], rule)
        down_copy.wait()
        total = None
        for r in range(down.shape[0]):
            mine = jnp.where(rule == r, critic_hidden, 0.0).astype(bf16)
            term = jnp.dot(mine, down[r], preferred_element_type=f32)
            total = term if total is None else total + term
        d0[...] = total
        send(d0, dh, d_send.at[0], d_recv.at[n_z], h_peer)

    def down_h():
        wait_for(dh, d_recv.at[n_z], d_send.at[0])
        both = d0[...] + dh[...]
        both = jnp.concatenate([both[:, :128], both[:, 128:]], axis=0).astype(bf16)
        d1[...] = both
        dz[z] = both
        for j in range(1, n_z):
            send(d1, dz.at[z], d_send.at[j], d_recv.at[z], z_peer[j])

    def down_z():
        for j in range(1, n_z):
            there = (z + j) % n_z
            wait_for(dz.at[there], d_recv.at[there], d_send.at[0])
        total = add([dz[a] for a in range(n_z)])
        critic_values[...] = jnp.concatenate([total[:docs], total[docs:]], axis=1).astype(bf16)

    mine = (y * NC + c) * NX + x

    def product(a, weights):
        return jnp.dot(both[a].reshape(NC * tokens, depth), weights[a], preferred_element_type=f32)

    def use_w(a):
        acc_kv[...] += product(a, wkv).reshape(acc_kv.shape)

    def use_q(a):
        acc_q[...] += product(a, wq).reshape(acc_q.shape)

    def kv_part():
        send(acc_kv.at[1 - c], part_kv, swap.at[2], swap.at[3], sib)

    def kv_own_kind():
        wait_for(part_kv, swap.at[3], swap.at[2])
        kv[kind, mine] = (acc_kv[c] + part_kv[...]).astype(bf16)
        send(kv.at[kind, mine], kv.at[kind, mine], kvz.at[0], kvz.at[1], z_mate)

    def other_kind():
        wait_for(kv.at[1 - kind, mine], kvz.at[1], kvz.at[0])

    def q_part():
        send(acc_q.at[1 - c], part_q, swap.at[4], swap.at[5], sib)

    def q_sum():
        wait_for(part_q, swap.at[5], swap.at[4])

    rows = QH_DEV * tokens
    chunk = NX * tokens
    inverse_root = 1.0 / math.sqrt(128)

    def attend(g):
        k_other(g)
        v_other(g)
        if g == 0:
            queries = (acc_q[c] + part_q[...]).astype(bf16)
            stacked[:tokens] = queries[:, :128]
            stacked[tokens:] = queries[:, 128:]
            maxima[...] = jnp.full_like(maxima, -1e30)
            totals[...] = jnp.zeros_like(totals)
            mixed[...] = jnp.zeros_like(mixed)
        chip_row = (y + FAR[g] + NY) % NY

        def step(i, carry):
            at = (chip_row * NC + i) * NX
            keys = kv[0, pl.ds(at, NX)].reshape(chunk, 128)
            values = kv[1, pl.ds(at, NX)].reshape(chunk, 128)
            position = lax.broadcasted_iota(jnp.int32, (rows, 1), 0) % tokens + first
            start = jnp.zeros((rows, 1), jnp.int32)
            for d in range(docs):
                start = jnp.maximum(start, jnp.where(ends[d] < position, ends[d] + 1, 0))
            found = lax.dot_general(
                stacked[...], keys, (((1,), (1,)), ((), ())), preferred_element_type=f32
            )
            there = lax.broadcasted_iota(jnp.int32, (1, chunk), 1)
            chip = chip_row * NX + lax.div(there, tokens)
            there = (chip * NC + i) * tokens + lax.rem(there, tokens)
            allowed = (there >= start) & (there <= position)
            found = jnp.where(allowed, found * inverse_root, -1e30)
            old = maxima[...]
            new = jnp.maximum(old, jnp.max(found, axis=1, keepdims=True))
            weights = jnp.where(allowed, jnp.exp(found - new[:, :1]), 0.0)
            keep = jnp.exp(old - new)
            maxima[...] = new
            totals[...] = totals[...] * keep + jnp.sum(weights, axis=1, keepdims=True)
            mixed[...] = mixed[...] * keep + jnp.dot(
                weights.astype(bf16), values, preferred_element_type=f32
            )
            return carry

        if g == 0:
            lax.fori_loop(0, NC, step, 0)
        else:

            @pl.when(chip_row < y)
            def _():
                lax.fori_loop(0, NC, step, 0)

    value_copy.wait()
    wq_copy.wait()
    waiting, ready = [], [False]

    def use(what, a):
        if ready[0]:
            what(a)
        else:
            waiting.append((what, a))

    stages = {
        "ends": end_rows, "norm": norm, "ey": end_rows_y, "ex": end_rows_x, "up": up_terms, "uy": up_y,
        "ux": up_x, "down": down_terms, "dh": down_h, "late": late, "both": other_rows, "kpart": kv_part,
        "kown": kv_own_kind, "z": other_kind, "qpart": q_part, "qown": q_sum,
        **{f"a{g}": functools.partial(attend, g) for g in range(4)}, "dz": down_z,
    }
    for step in SCHEDULE:
        if step in stages:
            stages[step]()
            if step == "both":
                ready[0] = True
                for what, a in waiting:
                    what(a)
            continue
        i = int(step[1:])
        if step[0] == "w":
            use(use_w, w_own(i))
        if step[0] == "q":
            use(use_q, q_own(i))
        if step[0] == "k":
            k_own(i)
        if step[0] == "v":
            v_own(i)
    out = (mixed[...] / totals[...]).astype(bf16)
    attention[:, :128] = out[:tokens]
    attention[:, 128:] = out[tokens:]
    for copy, when in sends:
        if when is None:
            copy.wait_send()
        else:
            pl.when(when)(copy.wait_send)


def hand_over(attention, critic_values, attention_out, critic_values_out):
    attention_out[...] = attention[...]
    critic_values_out[...] = critic_values[...]


def shards(
    hidden, norm_gain, w_query, w_key, w_value, doc_lengths, critic_up, critic_down, rule_ids
):
    tokens, width = hidden.shape
    depth, q_columns = w_query.shape
    rules, hidden_units, out_columns = critic_down.shape
    docs = doc_lengths.shape[0]
    n_seq = NY * NX * NC
    n_z = lax.axis_size("tp") // NH
    folded = (2 * docs, (hidden_units // 2 + 127) // 128 * 128)
    bf16, f32 = jnp.bfloat16, jnp.float32
    vmem, dma = pltpu.VMEM, pltpu.SemaphoreType.DMA
    anywhere = pl.BlockSpec(memory_space=pl.ANY)
    made = pl.pallas_call(
        kernel,
        out_shape=(
            jax.ShapeDtypeStruct((tokens, q_columns), bf16),
            jax.ShapeDtypeStruct((docs, out_columns), bf16),
        ),
        in_specs=[
            pl.BlockSpec(memory_space=pltpu.SMEM),
            pl.BlockSpec(memory_space=pltpu.SMEM),
            pl.BlockSpec(memory_space=pltpu.VMEM),
            *[anywhere] * 6,
        ],
        out_specs=(pl.BlockSpec(memory_space=pltpu.VMEM), pl.BlockSpec(memory_space=pltpu.VMEM)),
        scratch_shapes=[
            vmem((tokens, width), bf16),
            vmem((n_seq // NC, NC, tokens, depth), bf16),
            vmem((n_seq // NC, tokens, depth), bf16),
            vmem((n_seq // NC, depth, 128), bf16),
            vmem((n_seq // NC, depth, q_columns), bf16),
            vmem(critic_up.shape, bf16),
            vmem(critic_down.shape, bf16),
            vmem((2, n_seq, tokens, 128), bf16),
            vmem((NC, tokens, 128), f32),
            vmem((tokens, 128), f32),
            vmem((NC, tokens, q_columns), f32),
            vmem((tokens, q_columns), f32),
            vmem((QH_DEV * tokens, 128), bf16),
            *[vmem((QH_DEV * tokens, 128), f32)] * 3,
            vmem((NY, NX, NC * docs, depth), bf16),
            vmem((NY - 1, NX, NC * docs, depth), bf16),
            vmem((NX, NC * docs, depth), bf16),
            vmem((NX - 1, NC * docs, depth), bf16),
            vmem((NC * docs, depth), bf16),
            vmem((NC * docs, depth), bf16),
            vmem((docs, width), f32),
            vmem(folded, bf16),
            vmem((NY - 1, *folded), bf16),
            vmem(folded, bf16),
            vmem((NX - 1, *folded), bf16),
            vmem(folded, bf16),
            vmem(folded, bf16),
            vmem((docs, out_columns), f32),
            vmem((docs, out_columns), f32),
            vmem((2 * docs, out_columns // 2), bf16),
            vmem((n_z, 2 * docs, out_columns // 2), bf16),
            dma((5,)),
            *[dma((N_SENDS,)), dma((n_seq,))] * 4,
            dma((8,)),
            dma((8,)),
            dma((2,)),
            dma((6,)),
            dma((7,)),
            dma((7,)),
            dma((7,)),
            dma((7,)),
            dma((n_z,)),
            dma((n_z + 1,)),
        ],
        compiler_params=pltpu.CompilerParams(
            collective_id=0, has_side_effects=True, vmem_limit_bytes=60 * 1024 * 1024
        ),
        cost_estimate=pl.CostEstimate(
            flops=2 * 10**9, bytes_accessed=8 * 2**20, transcendentals=2**20
        ),
    )(
        doc_lengths, rule_ids, norm_gain, hidden, w_query, w_key, w_value,
        critic_up, critic_down,
    )
    inside = pl.BlockSpec(memory_space=pltpu.VMEM)
    return pl.pallas_call(
        hand_over,
        out_shape=tuple(jax.ShapeDtypeStruct(part.shape, part.dtype) for part in made),
        in_specs=[inside, inside],
        out_specs=(inside, inside),
    )(*made)


def solution(mesh):
    return jax.shard_map(
        shards,
        mesh=mesh,
        in_specs=(
            P("seq", None),
            P(),
            P("seq", "tp"),
            P("seq", None),
            P("seq", None),
            P(),
            P("seq", "tp"),
            P(None, "tp", "seq"),
            P(),
        ),
        out_specs=(P("seq", "tp"), P(None, "seq")),
        check_vma=False,
    )
```
